32 devices in a mesh: slab: 8 (over y, x, core), orb: 4 (over z).
Axes of the slice: x: 2, y: 2, z: 4, core: 2. Of those that a mesh axis runs over, the one named last changes fastest.
Arguments:
- inverses: bfloat16 [8, 4, 2, 8, 512, 512], P('slab', None, None, 'orb'), may hold values from -0.5 to 1.5
- coupling: bfloat16 [8, 2, 32, 3, 128, 128], P('slab', None, 'orb'), may hold values from -0.21875 to 0.21875
- pattern: int32 [8, 32, 3], P('slab', 'orb'), may hold values 0 or 1
- left_lead: bfloat16 [4, 2, 64, 4096], P(None, None, None, 'orb'), may hold values from -6 to 6
- right_lead: bfloat16 [4, 2, 64, 4096], P(None, None, None, 'orb'), may hold values from -6 to 6
- potential: float32 [8, 4096], P('slab', 'orb'), may hold values from -0.5 to 0.5
- fermi_weight: float32 [64], replicated, may hold values from 0.1 to 1
- energy_index: int32 [4], replicated, may hold values from 0 to 63
- owner_map: int32 [8, 512, 1], P('slab', 'orb'), may hold values from 0 to 7; in each aligned block of 128 rows (0 to 127, 128 to 255, ..., all dimensions but the last counted through in order) at most 16 rows name the same one
Outputs:
- green_carry: bfloat16 [8, 4, 2, 64, 4096], P('slab', None, None, None, 'orb')
- owner_rows: float32 [8, 8, 64, 8, 128], P('slab', None, 'orb')
The draws below stay inside these ranges and needn't reach their ends.
Inputs may be any that keep to these rules, and one draw needn't show every extreme that they name: `owner_map`: among the atoms of one device (aligned runs of 128 atoms of a slab) at most 16 name the same owner, and exactly 16 do in some run.
All inputs are finite; a program needn't handle non-finite values. No bound on the sum of `pattern` on one device may be relied on, other than what follows from the above.
Results may differ from the reference program's by a relative error of at most 0.04.
Values may be sent and summed in bfloat16 or wider, within the bound.
A program may use at most 128 MiB of HBM per device.

```python
import math
import jax
import jax.numpy as jnp
import numpy as np
from jax import lax

ORB = 4096
BLK = 128
GB = 512
NCOL = 64
NE = 4
NGRID = 64
ATOM_ORB = 8
SCAP = 16
SLABS = 8
N_SLAB = 8
N_ORB = 4


def draw_inverses(key, part):
    shape = (N_SLAB, NE, 2, ORB // GB, GB, GB)
    spread = math.sqrt(0.15 / GB)
    noise = jax.random.normal(key, shape, jnp.float32) * spread
    identity = jnp.eye(GB, dtype=jnp.float32)
    real_mask = (jnp.arange(2) == 0).astype(jnp.float32)
    return (noise + real_mask[None, None, :, None, None, None] * identity).astype(jnp.bfloat16)


def plant(array, rng, smallest, high):
    extent = array.shape
    spot = [jax.random.randint(jax.random.fold_in(rng, axis), (), 0, extent[axis]) for axis in range(len(extent))]
    array = array.at[tuple(spot)].set(smallest)
    longest = extent.index(max(extent))
    spot[longest] = (spot[longest] + 1) % extent[longest]
    return array.at[tuple(spot)].set(high)


def shard_levels(stream_key, shape, cuts, least, top_value):
    def one(axis_at, blocks):
        heights = jax.random.uniform(jax.random.fold_in(jax.random.fold_in(stream_key, 6), axis_at), (blocks,), jnp.float32, least / len(cuts), top_value / len(cuts))
        return jnp.repeat(jnp.exp(heights), shape[axis_at] // blocks).reshape((-1,) + (1,) * (len(shape) - axis_at - 1))

    gain = one(*cuts[0])
    for cut in cuts[1:]:
        gain = gain * one(*cut)
    return gain


def routed_block(rng, own, number, rows, count, top, bound, slope):
    order = jax.random.permutation(rng, count)
    heavy_load, common = portions_of(count, rows * top, bound, slope, True), portions_of(count, rows * top, bound, slope, False)
    places = jnp.arange(count)

    def named(lengths, offset_by):
        used = int((lengths > 0).sum())
        fixed = max(1, used // 4)
        passed = fixed + (places - fixed + offset_by * (used - fixed)) % max(1, count - fixed)
        return jnp.zeros((count,), jnp.int32).at[order[jnp.where(places < fixed, places, passed)]].set(jnp.asarray(lengths, jnp.int32))

    lengths = jnp.where(number % 4 == 0, named(heavy_load, number // 4), named(common, number - number // 4 - 1))
    mixed = jax.random.permutation(jax.random.fold_in(own, 3), count)
    giver, sink = mixed[0:count // 2 * 2:2], mixed[1:count // 2 * 2:2]
    margin = jnp.minimum(lengths[giver] - 1, bound - lengths[sink]) // 2
    margin = jnp.where((giver == order[0]) | (sink == order[0]) | (lengths[sink] == 0), 0, jnp.maximum(margin, 0))
    passed = jax.random.randint(jax.random.fold_in(own, 4), (count // 2,), 0, 1 << 20) % (margin + 1)
    lengths = lengths.at[giver].add(-passed).at[sink].add(passed)
    members = jnp.searchsorted(jnp.cumsum(lengths), jnp.arange(rows * top), side="right").astype(jnp.int32)
    grid = members.reshape(top, rows).T
    grid = grid[jax.random.permutation(jax.random.fold_in(own, 1), rows)]
    offset_by = jax.random.randint(jax.random.fold_in(own, 2), (rows, 1), 0, top)
    return jnp.take_along_axis(grid, (jnp.arange(top)[None, :] + offset_by) % top, axis=1)


def portions_of(count, total, most, skew, full):
    weights = [(1 << 20) // math.isqrt(grade ** skew) + 1 for grade in range(1, count + 1)]
    largest = most if full else min(most, max(-(-total // count), total * weights[0] // sum(weights)))
    least = 1 if total - largest >= count - 1 else 0
    counts, surplus = [largest] + [least] * (count - 1), total - largest - least * (count - 1)
    while surplus > 0:
        movable = [i for i in range(1, count) if counts[i] < largest] or [i for i in range(1, count) if counts[i] < most]
        mass, left = sum([weights[i] for i in movable]), surplus
        for i in movable:
            more = min(most - counts[i], max(1, left * weights[i] // mass), surplus)
            counts[i] = counts[i] + more
            surplus = surplus - more
    return np.array(counts)


def scatter_about(rng, extent, deviation, limit, shards=(), kind=jnp.bfloat16):
    level = shard_levels(rng, extent, shards, -0.22, 0.18) if shards else 1.0
    values = jax.random.normal(rng, extent, jnp.float32) * deviation * level
    return jnp.minimum(jnp.maximum(values, -limit), limit).astype(kind)


def setup_inputs(seed: int = 0) -> dict:
    key_list = jax.random.split(jax.random.key(seed), 10)
    inverses = draw_inverses(jax.random.fold_in(key_list[9], 71), 0)
    coupling = scatter_about(key_list[1], (SLABS, 2, ORB // BLK, 3, BLK, BLK), (6 * BLK) ** -0.5, 0.21875, ((0, 8), (2, 4)))
    pattern = plant((jax.random.randint(key_list[2], (SLABS, ORB // BLK, 3), 0, 3) < 2).astype(jnp.int32), jax.random.fold_in(key_list[2], 1), 0, 1)
    left_lead = scatter_about(key_list[3], (NE, 2, NCOL, ORB), 1.0, 6.0, ((3, 4),))
    right_lead = scatter_about(key_list[4], (NE, 2, NCOL, ORB), 1.0, 6.0, ((3, 4),))
    potential = jnp.clip(jax.random.uniform(key_list[5], (SLABS, ORB), jnp.float32, -0.5, 0.5) * shard_levels(key_list[5], (SLABS, ORB), ((0, 8), (1, 4)), -0.4, 0.0), -0.5, 0.5)
    fermi_weight = jnp.clip(jnp.exp(jax.random.uniform(key_list[6], (NGRID,), jnp.float32, math.log(0.1), math.log(1.0))), 0.1, 1.0)
    energy_index = plant(jax.random.randint(key_list[7], (NE,), 0, NGRID), jax.random.fold_in(key_list[7], 1), 0, NGRID - 1).astype(jnp.int32)
    owner_map_keys = jax.random.split(jax.random.fold_in(key_list[8], 1), SLABS * (ORB // ATOM_ORB) // (ORB // ATOM_ORB // N_ORB))
    owner_map_turns = jax.random.permutation(jax.random.fold_in(key_list[8], 3), SLABS * (ORB // ATOM_ORB) // (ORB // ATOM_ORB // N_ORB))
    owner_map = jax.vmap(lambda own, number: routed_block(jax.random.fold_in(key_list[8], 2), own, number, ORB // ATOM_ORB // N_ORB, N_SLAB, 1, SCAP, 2))(owner_map_keys, owner_map_turns).reshape((SLABS, ORB // ATOM_ORB, 1))
    return {"inverses": inverses, "coupling": coupling, "pattern": pattern, "left_lead": left_lead, "right_lead": right_lead, "potential": potential, "fermi_weight": fermi_weight, "energy_index": energy_index, "owner_map": owner_map}


def settle(value):
    return lax.optimization_barrier(value.astype(jnp.bfloat16))


def through_inverse(blocks, carry):
    energies, _, modes, orbitals = carry.shape
    block_count = blocks.shape[2]
    block_size = blocks.shape[3]
    real_part = blocks[:, 0].astype(jnp.float32)
    imag_part = blocks[:, 1].astype(jnp.float32)
    parted = carry.astype(jnp.float32).reshape(energies, 2, modes, block_count, block_size)

    def product(left_side, right_side):
        return jnp.einsum('ecgp,egop->ecgo', left_side, right_side, precision=lax.Precision.HIGHEST)

    real_out = product(parted[:, 0], real_part) - product(parted[:, 1], imag_part)
    imag_out = product(parted[:, 0], imag_part) + product(parted[:, 1], real_part)
    return jnp.stack([real_out, imag_out], 1).reshape(energies, 2, modes, orbitals)


def born_map(blocks, potential_row, carry):
    gained = settle(through_inverse(blocks, carry))
    mixed = settle(carry.astype(jnp.float32) + potential_row * gained.astype(jnp.float32))
    return through_inverse(blocks, mixed)


def masked_coupling(coupling_slab, pattern_slab):
    return coupling_slab.astype(jnp.float32) * pattern_slab[None, :, :, None, None].astype(jnp.float32)


def couple_rows(masked, carry):
    energies, _, modes, orbitals = carry.shape
    block_width = masked.shape[-1]
    nblocks = orbitals // block_width
    padded = jnp.pad(carry.astype(jnp.float32), ((0, 0), (0, 0), (0, 0), (block_width, block_width)))
    windows = jnp.stack([padded[..., offset * block_width: offset * block_width + orbitals] for offset in range(3)], 3)
    windows = windows.reshape(energies, 2, modes, 3, nblocks, block_width)

    def product(left_side, right_side):
        return jnp.einsum('ecdrp,rdop->ecro', left_side, right_side, precision=lax.Precision.HIGHEST)

    real_out = product(windows[:, 0], masked[0]) - product(windows[:, 1], masked[1])
    imag_out = product(windows[:, 0], masked[1]) + product(windows[:, 1], masked[0])
    return jnp.stack([real_out, imag_out], 1).reshape(energies, 2, modes, orbitals)


def couple_back(masked, carry):
    energies, _, modes, orbitals = carry.shape
    block_width = masked.shape[-1]
    nblocks = orbitals // block_width
    parted = carry.astype(jnp.float32).reshape(energies, 2, modes, nblocks, block_width)

    def product(left_side, right_side):
        return jnp.einsum('ecro,rdop->ecrdp', left_side, right_side, precision=lax.Precision.HIGHEST)

    real_out = product(parted[:, 0], masked[0]) + product(parted[:, 1], masked[1])
    imag_out = product(parted[:, 1], masked[0]) - product(parted[:, 0], masked[1])
    both = jnp.stack([real_out, imag_out], 1)
    spread = jnp.zeros((energies, 2, modes, orbitals + 2 * block_width), jnp.float32)
    for offset in range(3):
        piece = both[:, :, :, :, offset, :].reshape(energies, 2, modes, orbitals)
        spread = spread + jnp.pad(piece, ((0, 0), (0, 0), (0, 0), (offset * block_width, (2 - offset) * block_width)))
    return spread[..., block_width: block_width + orbitals]


def reference(inverses, coupling, pattern, left_lead, right_lead, potential, fermi_weight, energy_index, owner_map):
    carry_now = left_lead
    forward_rows = []
    for slab_index in range(N_SLAB):
        masked = masked_coupling(coupling[slab_index], pattern[slab_index])
        entering = settle(couple_rows(masked, carry_now))
        carry_now = settle(born_map(inverses[slab_index], potential[slab_index], entering))
        forward_rows.append(carry_now)
    entering = right_lead
    green_rows = [None] * N_SLAB
    for slab_index in range(N_SLAB - 1, -1, -1):
        green_now = settle(forward_rows[slab_index].astype(jnp.float32) + born_map(inverses[slab_index], potential[slab_index], entering))
        green_rows[slab_index] = green_now
        if slab_index > 0:
            masked = masked_coupling(coupling[slab_index], pattern[slab_index])
            entering = settle(couple_back(masked, green_now))
    green_carry = jnp.stack(green_rows, 0)

    grid_points = jnp.arange(NGRID, dtype=jnp.int32)
    weights = jnp.sum(jnp.where(grid_points[None, :] == energy_index[:, None], fermi_weight[None, :], 0.0), 1)
    nblocks = ORB // BLK
    parted = green_carry.astype(jnp.float32).reshape(N_SLAB, NE, 2, NCOL, nblocks, BLK)
    inner_sum = jnp.einsum('seqcbo,seqcbp->sebop', parted, parted, precision=lax.Precision.HIGHEST)
    response = jnp.einsum('e,sebop->sbop', weights, inner_sum, precision=lax.Precision.HIGHEST) / (2.0 * NCOL)
    atoms_run = ORB // ATOM_ORB // N_ORB
    payload = response.reshape(N_SLAB, N_ORB, atoms_run, ATOM_ORB, BLK)

    owners = owner_map[:, :, 0].reshape(N_SLAB, N_ORB, atoms_run)
    targets = jnp.arange(N_SLAB, dtype=jnp.int32)
    matches = (owners[..., None] == targets).astype(jnp.int32)
    ranking = jnp.sum((jnp.cumsum(matches, 2) - 1) * matches, 3)
    sources = jnp.broadcast_to(jnp.arange(N_SLAB, dtype=jnp.int32)[:, None, None], owners.shape)
    slots = jnp.arange(N_ORB, dtype=jnp.int32)[None, :, None] * SCAP + ranking
    owner_rows = jnp.zeros((N_SLAB, N_SLAB, N_ORB * SCAP, ATOM_ORB, BLK), jnp.float32)
    owner_rows = owner_rows.at[owners, sources, slots].set(payload)
    return green_carry, owner_rows
```

```python
import functools

import jax
import jax.numpy as jnp
from jax import lax
from jax.experimental import pallas as pl
from jax.experimental.pallas import tpu as pltpu
from jax.sharding import PartitionSpec as P

ATOM_ORB = 8
SCAP = 16
F32 = jnp.float32
BF16 = jnp.bfloat16


def turned(u, conj):
    half = u.shape[0] // 2
    r, i = u[:half], u[half:]
    return jnp.concatenate([i, -r] if conj else [-i, r], 0)


def coupled(window, weight, conj):
    both = jnp.dot(window, weight, preferred_element_type=F32)
    half, width = both.shape[0] // 2, both.shape[1] // 2
    rr, ri = both[:half, :width], both[:half, width:]
    ir, ii = both[half:, :width], both[half:, width:]
    if conj:
        out = [rr + ii, ir - ri]
    else:
        out = [rr - ii, ri + ir]
    return jnp.concatenate(out, 0).astype(BF16)


def kernel(
    dims,
    inv, mf, mb, left, right, pot, fermi, eidx, own_row, own_col,
    gout, rows_out,
    ginv, xf, gf, xs, bb, stage, resp, sel, picked, sb, rb,
    inv_sem, fs, fr, bs, br, cs, cr, ls, ts, tr,
):
    S, Q, E, W, NB, BW, NG, GB = dims
    s = lax.axis_index("slab")
    q = lax.axis_index("orb")
    rows = xf.shape[1]
    first, last = s == 0, s == S - 1
    low, high = q == 0, q == Q - 1

    def to(src, dst, ssem, rsem, ds, dq):
        return pltpu.make_async_remote_copy(
            src_ref=src, dst_ref=dst, send_sem=ssem, recv_sem=rsem,
            device_id={"slab": s + ds, "orb": q + dq},
            device_id_type=pl.DeviceIdType.MESH,
        )

    def here(src, dst, sem):
        return pltpu.make_async_copy(src, dst, sem)

    def inv_copy(e):
        return here(inv.at[e], ginv.at[e], inv_sem.at[e])

    def main(buf, e, g):
        return buf.at[e, :, pl.ds(BW + g * GB, GB)]

    def halo(buf, e, side):
        return buf.at[e, :, pl.ds(0 if side == 0 else BW + W, BW)]

    def edge(src, e, side):
        return src.at[e, :, pl.ds(0 if side == 0 else W - BW, BW)]

    def coupling_copies():
        out = [(None, to(mb.at[:, 1], bb.at[:, 1], cs.at[0], cr.at[0], -1, 0))]
        n = NB - 1
        out.append((None, to(mb.at[pl.ds(1, n), 0], bb.at[pl.ds(0, n), 2], cs.at[1], cr.at[1], -1, 0)))
        out.append((None, to(mb.at[pl.ds(0, n), 2], bb.at[pl.ds(1, n), 0], cs.at[2], cr.at[2], -1, 0)))
        out.append((~low, to(mb.at[0, 0], bb.at[NB - 1, 2], cs.at[3], cr.at[3], -1, -1)))
        out.append((~high, to(mb.at[NB - 1, 2], bb.at[0, 0], cs.at[4], cr.at[4], -1, 1)))
        return out

    def wave_copies(src, dst, e, ssem, rsem, ds):
        out = []
        for g in range(NG):
            out.append((None, g, to(src.at[e, :, pl.ds(g * GB, GB)], main(dst, e, g), ssem.at[e, g], rsem.at[e, g], ds, 0)))
        out.append((~low, 0, to(edge(src, e, 0), halo(dst, e, 1), ssem.at[e, NG], rsem.at[e, NG + 1], ds, -1)))
        out.append((~high, NG - 1, to(edge(src, e, 1), halo(dst, e, 0), ssem.at[e, NG + 1], rsem.at[e, NG], ds, 1)))
        return out

    def lead_copies(e):
        return [
            (~low, to(edge(left, e, 0), halo(xf, e, 1), ls.at[e, 0], fr.at[e, NG + 1], 0, -1)),
            (~high, to(edge(left, e, 1), halo(xf, e, 0), ls.at[e, 1], fr.at[e, NG], 0, 1)),
        ]

    def guarded(cond, act):
        if cond is None:
            act()
        else:
            pl.when(cond)(act)

    def await_wave(buf, e, rsem, halos):
        for g in range(NG):
            here(main(buf, e, g), main(buf, e, g), rsem.at[e, g]).wait()
        if halos:
            for side, edge_here in ((0, low), (1, high)):
                h = halo(buf, e, side)
                pl.when(~edge_here)(lambda h=h, side=side: here(h, h, rsem.at[e, NG + side]).wait())

    def each_energy(body):
        def step(e, carry):
            body(e)
            return carry

        lax.fori_loop(0, E, step, 0)

    @each_energy
    def _(e):
        inv_copy(e).start()

    @pl.when(first)
    def _():
        @each_energy
        def _(e):
            for g in range(NG):
                here(left.at[e, :, pl.ds(g * GB, GB)], main(xf, e, g), fr.at[e, g]).start()
            for cond, copy in lead_copies(e):
                guarded(cond, copy.start)

    @pl.when(last)
    def _():
        @each_energy
        def _(e):
            for g in range(NG):
                here(right.at[e, :, pl.ds(g * GB, GB)], main(gf, e, g), br.at[e, g]).start()

    @pl.when(~first)
    def _():
        for cond, copy in coupling_copies():
            guarded(cond, copy.start)

    zero = jnp.zeros((E, rows, BW), BF16)
    zero_block = jnp.zeros((BW, 2 * BW), BF16)

    @pl.when(low)
    def _():
        xf[:, :, pl.ds(0, BW)] = zero
        gf[:, :, pl.ds(0, BW)] = zero
        bb[0, 0] = zero_block

    @pl.when(high)
    def _():
        xf[:, :, pl.ds(BW + W, BW)] = zero
        gf[:, :, pl.ds(BW + W, BW)] = zero
        bb[NB - 1, 2] = zero_block

    resp[...] = jnp.zeros(resp.shape, F32)

    atoms = own_row.shape[1]
    earlier = lax.broadcasted_iota(jnp.int32, (atoms, atoms), 0) < lax.broadcasted_iota(jnp.int32, (atoms, atoms), 1)
    same = own_col[...] == own_row[...]
    rank = jnp.sum((same & earlier).astype(F32), 0, keepdims=True)
    place = lax.broadcasted_iota(jnp.int32, (S * SCAP, atoms), 0)
    rank_i = rank.astype(jnp.int32)
    wanted = own_row[...] * SCAP + rank_i
    sel[...] = jnp.where(place == wanted, 1.0, 0.0).astype(BF16)

    def through(e, g, u):
        dn = (((1,), (1,)), ((), ()))
        return lax.dot_general(u, ginv[e, 0, g], dn, preferred_element_type=F32) + lax.dot_general(
            turned(u, False), ginv[e, 1, g], dn, preferred_element_type=F32
        )

    def born(e, g):
        u = stage[:, pl.ds(g * GB, GB)]
        gain = through(e, g, u).astype(BF16).astype(F32)
        mix = (u.astype(F32) + pot[:, pl.ds(g * GB, GB)] * gain).astype(BF16)
        return through(e, g, mix)

    def couple(buf, e, weights, conj):
        for b in range(NB):
            window = buf[e, :, pl.ds(b * BW, 3 * BW)]
            stage[:, pl.ds(b * BW, BW)] = coupled(window, weights[b].reshape(3 * BW, 2 * BW), conj)

    def forward(e):
        inv_copy(e).wait()
        await_wave(xf, e, fr, True)
        couple(xf, e, mf, False)
        copies = wave_copies(xs, xf, e, fs, fr, 1)
        for g in range(NG):
            xs[e, :, pl.ds(g * GB, GB)] = born(e, g).astype(BF16)

            @pl.when(~last)
            def _():
                for cond, after, copy in copies:
                    if after == g:
                        guarded(cond, copy.start)

    each_energy(forward)

    @pl.when(~last)
    def _():
        for i, region in enumerate((bb.at[:, 1], bb.at[pl.ds(0, NB - 1), 2], bb.at[pl.ds(1, NB - 1), 0])):
            here(region, region, cr.at[i]).wait()
        pl.when(~high)(lambda: here(bb.at[NB - 1, 2], bb.at[NB - 1, 2], cr.at[3]).wait())
        pl.when(~low)(lambda: here(bb.at[0, 0], bb.at[0, 0], cr.at[4]).wait())

    def backward(e):
        @pl.when(last)
        def _():
            await_wave(gf, e, br, False)
            stage[...] = gf[e, :, pl.ds(BW, W)]

        @pl.when(~last)
        def _():
            await_wave(gf, e, br, True)
            couple(gf, e, bb, True)

        copies = wave_copies(gout, gf, e, bs, br, -1)
        for g in range(NG):
            cols = pl.ds(g * GB, GB)
            gout[e, :, cols] = (xs[e, :, cols].astype(F32) + born(e, g)).astype(BF16)

            @pl.when(~first)
            def _():
                for cond, after, copy in copies:
                    if after == g:
                        guarded(cond, copy.start)

        weight = fermi[eidx[e]]
        for b in range(NB):
            a = gout[e, :, pl.ds(b * BW, BW)]
            gram = lax.dot_general(a, a, (((0,), (0,)), ((), ())), preferred_element_type=F32)
            resp[pl.ds(b * BW, BW), :] += weight * gram

    each_energy(backward)

    for x in range(ATOM_ORB):
        part = (resp[pl.ds(x, atoms, stride=ATOM_ORB), :] * (1.0 / rows)).astype(BF16)
        picked[pl.ds(x, S * SCAP, stride=ATOM_ORB), :] = jnp.dot(sel[...], part, preferred_element_type=F32)
    sb[...] = picked[...].reshape(sb.shape).astype(BF16)

    def tail(k):
        other = lax.rem(s + k, S)
        return pltpu.make_async_remote_copy(
            src_ref=sb.at[other], dst_ref=rb.at[s], send_sem=ts.at[k], recv_sem=tr.at[k],
            device_id={"slab": other, "orb": q}, device_id_type=pl.DeviceIdType.MESH,
        )

    for k in range(1, S):
        tail(k).start()
    rb[s] = sb[s]

    @pl.when(~first)
    def _():
        for cond, copy in coupling_copies():
            guarded(cond, copy.wait_send)

        @each_energy
        def _(e):
            for cond, _, copy in wave_copies(gout, gf, e, bs, br, -1):
                guarded(cond, copy.wait_send)

    @pl.when(first)
    def _():
        @each_energy
        def _(e):
            for cond, copy in lead_copies(e):
                guarded(cond, copy.wait_send)

    @pl.when(~last)
    def _():
        @each_energy
        def _(e):
            for cond, _, copy in wave_copies(xs, xf, e, fs, fr, 1):
                guarded(cond, copy.wait_send)

    for k in range(1, S):
        tail(k).wait_send()
    for k in range(1, S):
        source = lax.rem(s + S - k, S)
        here(rb.at[source], rb.at[source], tr.at[k]).wait()
    rows_out[...] = rb[...].astype(F32)


def shards(
    inverses, coupling, pattern, left_lead, right_lead, potential, fermi_weight, energy_index, owner_map
):
    S, Q = lax.axis_size("slab"), lax.axis_size("orb")
    E, _, modes, W = left_lead.shape
    NB, BW = coupling.shape[2], coupling.shape[-1]
    NG, GB = inverses.shape[3], inverses.shape[4]
    rows = 2 * modes
    atoms = owner_map.shape[1]
    masked = coupling[0] * pattern[0][None, :, :, None, None].astype(BF16)
    mb = masked.transpose(1, 2, 3, 0, 4).reshape(NB, 3, BW, 2 * BW)
    mf = masked.transpose(1, 2, 4, 0, 3).reshape(NB, 3, BW, 2 * BW)
    owners = owner_map.reshape(atoms)
    vm = pl.BlockSpec(memory_space=pltpu.VMEM)
    sm = pl.BlockSpec(memory_space=pltpu.SMEM)
    hbm = pl.BlockSpec(memory_space=pl.ANY)
    dma = pltpu.SemaphoreType.DMA
    green, received = pl.pallas_call(
        functools.partial(kernel, (S, Q, E, W, NB, BW, NG, GB)),
        out_shape=(
            jax.ShapeDtypeStruct((E, rows, W), BF16),
            jax.ShapeDtypeStruct((S, SCAP * ATOM_ORB, BW), F32),
        ),
        in_specs=[hbm, vm, vm, hbm, hbm, vm, sm, sm, vm, vm],
        out_specs=(vm, vm),
        scratch_shapes=[
            pltpu.VMEM((E, 2, NG, GB, GB), BF16),
            pltpu.VMEM((E, rows, W + 2 * BW), BF16),
            pltpu.VMEM((E, rows, W + 2 * BW), BF16),
            pltpu.VMEM((E, rows, W), BF16),
            pltpu.VMEM((NB, 3, BW, 2 * BW), BF16),
            pltpu.VMEM((rows, W), BF16),
            pltpu.VMEM((W, BW), F32),
            pltpu.VMEM((S * SCAP, atoms), BF16),
            pltpu.VMEM((S * SCAP * ATOM_ORB, BW), F32),
            pltpu.VMEM((S, SCAP * ATOM_ORB, BW), BF16),
            pltpu.VMEM((S, SCAP * ATOM_ORB, BW), BF16),
            dma((E,)),
            dma((E, NG + 2)),
            dma((E, NG + 2)),
            dma((E, NG + 2)),
            dma((E, NG + 2)),
            dma((5,)),
            dma((5,)),
            dma((E, 2)),
            dma((S,)),
            dma((S,)),
        ],
        compiler_params=pltpu.CompilerParams(has_side_effects=True, vmem_limit_bytes=48 * 2**20),
    )(
        inverses[0],
        mf,
        mb,
        left_lead.reshape(E, rows, W),
        right_lead.reshape(E, rows, W),
        potential,
        fermi_weight,
        energy_index,
        owners.reshape(1, atoms),
        owners.reshape(atoms, 1),
    )
    return (
        green.reshape(1, E, 2, modes, W),
        received.reshape(1, S, SCAP, ATOM_ORB, BW),
    )


def solution(mesh):
    in_specs = (
        P("slab", None, None, "orb", None, None),
        P("slab", None, "orb", None, None, None),
        P("slab", "orb", None),
        P(None, None, None, "orb"),
        P(None, None, None, "orb"),
        P("slab", "orb"),
        P(),
        P(),
        P("slab", "orb", None),
    )
    out_specs = (P("slab", None, None, None, "orb"), P("slab", None, "orb", None, None))
    return jax.shard_map(shards, mesh=mesh, in_specs=in_specs, out_specs=out_specs, check_vma=False)
```

```python
import functools

import jax
import jax.numpy as jnp
from jax import lax
from jax.experimental import pallas as pl
from jax.experimental.pallas import tpu as pltpu
from jax.sharding import PartitionSpec as P

ATOM_ORB = 8
SCAP = 16
LAG = 2
F32 = jnp.float32
BF16 = jnp.bfloat16


def turned(u, conj):
    half = u.shape[0] // 2
    r, i = u[:half], u[half:]
    return jnp.concatenate([i, -r] if conj else [-i, r], 0)


def coupled(window, weight, conj):
    both = jnp.dot(window, weight, preferred_element_type=F32)
    half, width = both.shape[0] // 2, both.shape[1] // 2
    rr, ri = both[:half, :width], both[:half, width:]
    ir, ii = both[half:, :width], both[half:, width:]
    if conj:
        out = [rr + ii, ir - ri]
    else:
        out = [rr - ii, ri + ir]
    return jnp.concatenate(out, 0).astype(BF16)


def kernel(
    dims,
    inv, coup, left, right, pot, pattern, fermi, eidx, own_row,
    gout, rows_out,
    ginv, gturn, xf, gf, xs, mf, mb, bb, stage, resp, sel, picked, sb, rb,
    inv_sem, fs, fr, bs, br, cs, cr, ls, ts, tr,
):
    S, Q, E, W, NB, BW, NG, GB = dims
    s = lax.axis_index("slab")
    q = lax.axis_index("orb")
    rows = xf.shape[1]
    first, last = s == 0, s == S - 1
    low, high = q == 0, q == Q - 1

    def to(src, dst, ssem, rsem, ds, dq):
        return pltpu.make_async_remote_copy(
            src_ref=src, dst_ref=dst, send_sem=ssem, recv_sem=rsem,
            device_id={"slab": s + ds, "orb": q + dq},
            device_id_type=pl.DeviceIdType.MESH,
        )

    def here(src, dst, sem):
        return pltpu.make_async_copy(src, dst, sem)

    def inv_copy(e):
        return here(inv.at[e], ginv.at[e], inv_sem.at[e])

    pieces = [(0, 0, GB)]
    for g in range(1, NG):
        pieces += [(g, g * GB, BW), (g, g * GB + BW, GB - BW)]
    NP = len(pieces)

    def main(buf, e, p):
        return buf.at[e, :, pl.ds(BW + pieces[p][1], pieces[p][2])]

    def cut(src, e, p):
        return src.at[e, :, pl.ds(pieces[p][1], pieces[p][2])]

    def halo(buf, e, side):
        return buf.at[e, :, pl.ds(0 if side == 0 else BW + W, BW)]

    def edge(src, e, side):
        return src.at[e, :, pl.ds(0 if side == 0 else W - BW, BW)]

    early = s < 2

    def coupling_copies():
        out = [(None, to(mb.at[:, 1], bb.at[:, 1], cs.at[0], cr.at[0], -1, 0))]
        n = NB - 1
        out.append((None, to(mb.at[pl.ds(1, n), 0], bb.at[pl.ds(0, n), 2], cs.at[1], cr.at[1], -1, 0)))
        out.append((None, to(mb.at[pl.ds(0, n), 2], bb.at[pl.ds(1, n), 0], cs.at[2], cr.at[2], -1, 0)))
        out.append((~low, to(mb.at[0, 0], bb.at[NB - 1, 2], cs.at[3], cr.at[3], -1, -1)))
        out.append((~high, to(mb.at[NB - 1, 2], bb.at[0, 0], cs.at[4], cr.at[4], -1, 1)))
        return out

    def wave_copies(src, dst, e, ssem, rsem, ds):
        out = [(~high, NG - 1, to(edge(src, e, 1), halo(dst, e, 0), ssem.at[e, NP + 1], rsem.at[e, NP], ds, 1))]
        for p in range(NP):
            out.append((None, pieces[p][0], to(cut(src, e, p), main(dst, e, p), ssem.at[e, p], rsem.at[e, p], ds, 0)))
        out.append((~low, 0, to(edge(src, e, 0), halo(dst, e, 1), ssem.at[e, NP], rsem.at[e, NP + 1], ds, -1)))
        return out

    def lead_copies(e):
        return [
            (~low, to(edge(left, e, 0), halo(xf, e, 1), ls.at[e, 0], fr.at[e, NP + 1], 0, -1)),
            (~high, to(edge(left, e, 1), halo(xf, e, 0), ls.at[e, 1], fr.at[e, NP], 0, 1)),
        ]

    def guarded(cond, act):
        if cond is None:
            act()
        else:
            pl.when(cond)(act)

    def await_pieces(buf, e, rsem, g):
        need = [2 * g] + ([2 * g + 1] if g + 1 < NG else [])
        for p in need:
            here(main(buf, e, p), main(buf, e, p), rsem.at[e, p]).wait()

    def await_halos(buf, e, rsem, g):
        for side, at, edge_here in ((0, 0, low), (1, NG - 1, high)):
            if g == at:
                h = halo(buf, e, side)
                pl.when(~edge_here)(lambda h=h, side=side: here(h, h, rsem.at[e, NP + side]).wait())

    def each_energy(body):
        def step(e, carry):
            body(e)
            return carry

        lax.fori_loop(0, E, step, 0)

    @each_energy
    def _(e):
        inv_copy(e).start()

    @pl.when(first)
    def _():
        @each_energy
        def _(e):
            for p in range(NP):
                here(cut(left, e, p), main(xf, e, p), fr.at[e, p]).start()
            for cond, copy in lead_copies(e):
                guarded(cond, copy.start)

    @pl.when(last)
    def _():
        @each_energy
        def _(e):
            for p in range(NP):
                here(cut(right, e, p), main(gf, e, p), br.at[e, p]).start()

    def mask_row(r, carry):
        for d in range(3):
            present = pattern[r * 3 + d].astype(F32)
            for c in range(2):
                block = (coup[c, r, d].astype(F32) * present).astype(BF16)
                mb[r, d, :, pl.ds(c * BW, BW)] = block
                mf[r, d, :, pl.ds(c * BW, BW)] = block.T
        return carry

    lax.fori_loop(0, NB, mask_row, 0)

    @pl.when(~first)
    def _():
        for cond, copy in coupling_copies():
            guarded(cond, copy.start)

    def turn_inverses(e):
        def turn(k, carry):
            gturn[e, k // NG, k % NG] = ginv[e, k // NG, k % NG].T
            return carry

        lax.fori_loop(0, 2 * NG, turn, 0)

    zero = jnp.zeros((E, rows, BW), BF16)
    zero_block = jnp.zeros((BW, 2 * BW), BF16)

    @pl.when(low)
    def _():
        xf[:, :, pl.ds(0, BW)] = zero
        gf[:, :, pl.ds(0, BW)] = zero
        bb[0, 0] = zero_block

    @pl.when(high)
    def _():
        xf[:, :, pl.ds(BW + W, BW)] = zero
        gf[:, :, pl.ds(BW + W, BW)] = zero
        bb[NB - 1, 2] = zero_block

    resp[...] = jnp.zeros(resp.shape, F32)

    atoms = own_row.shape[1]
    earlier = lax.broadcasted_iota(jnp.int32, (atoms, atoms), 0) < lax.broadcasted_iota(jnp.int32, (atoms, atoms), 1)
    eye = lax.broadcasted_iota(jnp.int32, (atoms, atoms), 0) == lax.broadcasted_iota(jnp.int32, (atoms, atoms), 1)
    own_col = jnp.sum(jnp.where(eye, own_row[...].astype(F32), 0.0), 1, keepdims=True)
    same = own_col == own_row[...].astype(F32)
    rank = jnp.sum((same & earlier).astype(F32), 0, keepdims=True)
    place = lax.broadcasted_iota(jnp.int32, (S * SCAP, atoms), 0)
    rank_i = rank.astype(jnp.int32)
    wanted = own_row[...] * SCAP + rank_i
    sel[...] = jnp.where(place == wanted, 1.0, 0.0).astype(BF16)

    def born(e, raw, g):
        held = ginv if raw else gturn
        dn = (((1,), (1 if raw else 0,)), ((), ()))

        def through(u):
            return lax.dot_general(u, held[e, 0, g], dn, preferred_element_type=F32) + lax.dot_general(
                turned(u, False), held[e, 1, g], dn, preferred_element_type=F32
            )

        u = stage[:, pl.ds(g * GB, GB)]
        gain = through(u).astype(BF16).astype(F32)
        mix = (u.astype(F32) + pot[:, pl.ds(g * GB, GB)] * gain).astype(BF16)
        return through(mix)

    def couple(buf, e, weights, g, conj):
        per = GB // BW
        for b in range(g * per, (g + 1) * per):
            window = buf[e, :, pl.ds(b * BW, 3 * BW)]
            stage[:, pl.ds(b * BW, BW)] = coupled(window, weights[b].reshape(3 * BW, 2 * BW), conj)

    def send(copies, g, cond):
        @pl.when(cond)
        def _():
            for c, after, copy in copies:
                if after == g:
                    guarded(c, copy.start)

    @pl.when(~early)
    def _():
        @each_energy
        def _(e):
            inv_copy(e).wait()
            turn_inverses(e)

    def forward(e, raw):
        if raw:
            inv_copy(e).wait()
        copies = wave_copies(xs, xf, e, fs, fr, 1)
        for g in range(NG):
            await_pieces(xf, e, fr, g)
            await_halos(xf, e, fr, g)
            couple(xf, e, mf, g, False)
            xs[e, :, pl.ds(g * GB, GB)] = born(e, raw, g).astype(BF16)
            send(copies, g, ~last)

    def backward(e):
        @pl.when(~last & (e == 0))
        def _():
            for i, region in enumerate((bb.at[:, 1], bb.at[pl.ds(0, NB - 1), 2], bb.at[pl.ds(1, NB - 1), 0])):
                here(region, region, cr.at[i]).wait()
            pl.when(~high)(lambda: here(bb.at[NB - 1, 2], bb.at[NB - 1, 2], cr.at[3]).wait())
            pl.when(~low)(lambda: here(bb.at[0, 0], bb.at[0, 0], cr.at[4]).wait())

        copies = wave_copies(gout, gf, e, bs, br, -1)
        for g in range(NG):
            cols = pl.ds(g * GB, GB)
            await_pieces(gf, e, br, g)

            @pl.when(last)
            def _():
                stage[:, cols] = gf[e, :, pl.ds(BW + g * GB, GB)]

            @pl.when(~last)
            def _():
                await_halos(gf, e, br, g)
                couple(gf, e, bb, g, True)

            gout[e, :, cols] = (xs[e, :, cols].astype(F32) + born(e, False, g)).astype(BF16)
            send(copies, g, ~first)

        weight = fermi[eidx[e]]
        for b in range(NB):
            a = gout[e, :, pl.ds(b * BW, BW)]
            gram = lax.dot_general(a, a, (((0,), (0,)), ((), ())), preferred_element_type=F32)
            resp[pl.ds(b * BW, BW), :] += weight * gram

    lag = jnp.where(last, 0, jnp.where(s == S - 2, min(LAG, E), E))

    def slot(t, carry):
        e = lax.rem(t, E)
        pl.when((t < E) & early)(lambda: forward(e, True))
        pl.when((t < E) & ~early)(lambda: forward(e, False))
        pl.when((t == E) & early)(lambda: each_energy(turn_inverses))
        pl.when((t >= lag) & (t < lag + E))(lambda: backward(lax.rem(t + 2 * E - lag, E)))
        return carry

    lax.fori_loop(0, 2 * E, slot, 0)

    for x in range(ATOM_ORB):
        part = (resp[pl.ds(x, atoms, stride=ATOM_ORB), :] * (1.0 / rows)).astype(BF16)
        picked[pl.ds(x, S * SCAP, stride=ATOM_ORB), :] = jnp.dot(sel[...], part, preferred_element_type=F32)
    sb[...] = picked[...].reshape(sb.shape).astype(BF16)

    def tail(k):
        other = lax.rem(s + k, S)
        return pltpu.make_async_remote_copy(
            src_ref=sb.at[other], dst_ref=rb.at[s], send_sem=ts.at[k], recv_sem=tr.at[k],
            device_id={"slab": other, "orb": q}, device_id_type=pl.DeviceIdType.MESH,
        )

    for k in range(1, S):
        tail(k).start()
    rb[s] = sb[s]

    @pl.when(~first)
    def _():
        for cond, copy in coupling_copies():
            guarded(cond, copy.wait_send)

        @each_energy
        def _(e):
            for cond, _, copy in wave_copies(gout, gf, e, bs, br, -1):
                guarded(cond, copy.wait_send)

    @pl.when(first)
    def _():
        @each_energy
        def _(e):
            for cond, copy in lead_copies(e):
                guarded(cond, copy.wait_send)

    @pl.when(~last)
    def _():
        @each_energy
        def _(e):
            for cond, _, copy in wave_copies(xs, xf, e, fs, fr, 1):
                guarded(cond, copy.wait_send)

    for k in range(1, S):
        tail(k).wait_send()
    for k in range(1, S):
        source = lax.rem(s + S - k, S)
        here(rb.at[source], rb.at[source], tr.at[k]).wait()
    rows_out[...] = rb[...].astype(F32)


def shards(
    inverses, coupling, pattern, left_lead, right_lead, potential, fermi_weight, energy_index, owner_map
):
    S, Q = lax.axis_size("slab"), lax.axis_size("orb")
    E, _, modes, W = left_lead.shape
    NB, BW = coupling.shape[2], coupling.shape[-1]
    NG, GB = inverses.shape[3], inverses.shape[4]
    rows = 2 * modes
    atoms = owner_map.shape[1]
    owners = owner_map.reshape(atoms)
    vm = pl.BlockSpec(memory_space=pltpu.VMEM)
    sm = pl.BlockSpec(memory_space=pltpu.SMEM)
    hbm = pl.BlockSpec(memory_space=pl.ANY)
    dma = pltpu.SemaphoreType.DMA
    green, received = pl.pallas_call(
        functools.partial(kernel, (S, Q, E, W, NB, BW, NG, GB)),
        out_shape=(
            jax.ShapeDtypeStruct((E, rows, W), BF16),
            jax.ShapeDtypeStruct((S, SCAP * ATOM_ORB, BW), F32),
        ),
        in_specs=[hbm, vm, hbm, hbm, vm, sm, sm, sm, vm],
        out_specs=(vm, vm),
        scratch_shapes=[
            pltpu.VMEM((E, 2, NG, GB, GB), BF16),
            pltpu.VMEM((E, 2, NG, GB, GB), BF16),
            pltpu.VMEM((E, rows, W + 2 * BW), BF16),
            pltpu.VMEM((E, rows, W + 2 * BW), BF16),
            pltpu.VMEM((E, rows, W), BF16),
            pltpu.VMEM((NB, 3, BW, 2 * BW), BF16),
            pltpu.VMEM((NB, 3, BW, 2 * BW), BF16),
            pltpu.VMEM((NB, 3, BW, 2 * BW), BF16),
            pltpu.VMEM((rows, W), BF16),
            pltpu.VMEM((W, BW), F32),
            pltpu.VMEM((S * SCAP, atoms), BF16),
            pltpu.VMEM((S * SCAP * ATOM_ORB, BW), F32),
            pltpu.VMEM((S, SCAP * ATOM_ORB, BW), BF16),
            pltpu.VMEM((S, SCAP * ATOM_ORB, BW), BF16),
            dma((E,)),
            dma((E, 2 * NG + 1)),
            dma((E, 2 * NG + 1)),
            dma((E, 2 * NG + 1)),
            dma((E, 2 * NG + 1)),
            dma((5,)),
            dma((5,)),
            dma((E, 2)),
            dma((S,)),
            dma((S,)),
        ],
        compiler_params=pltpu.CompilerParams(has_side_effects=True, vmem_limit_bytes=48 * 2**20),
    )(
        inverses[0],
        coupling[0],
        left_lead.reshape(E, rows, W),
        right_lead.reshape(E, rows, W),
        potential,
        pattern.reshape(NB * 3),
        fermi_weight,
        energy_index,
        owners.reshape(1, atoms),
    )
    return (
        green.reshape(1, E, 2, modes, W),
        received.reshape(1, S, SCAP, ATOM_ORB, BW),
    )


def solution(mesh):
    in_specs = (
        P("slab", None, None, "orb", None, None),
        P("slab", None, "orb", None, None, None),
        P("slab", "orb", None),
        P(None, None, None, "orb"),
        P(None, None, None, "orb"),
        P("slab", "orb"),
        P(),
        P(),
        P("slab", "orb", None),
    )
    out_specs = (P("slab", None, None, None, "orb"), P("slab", None, "orb", None, None))
    return jax.shard_map(shards, mesh=mesh, in_specs=in_specs, out_specs=out_specs, check_vma=False)
```

```python
import functools

import jax
import jax.numpy as jnp
from jax import lax
from jax.experimental import pallas as pl
from jax.experimental.pallas import tpu as pltpu
from jax.sharding import PartitionSpec as P

ATOM_ORB = 8
SCAP = 16
LAG = 2
F32 = jnp.float32
BF16 = jnp.bfloat16


def turned(u, conj):
    half = u.shape[0] // 2
    r, i = u[:half], u[half:]
    return jnp.concatenate([i, -r] if conj else [-i, r], 0)


def coupled(window, weight, conj):
    both = jnp.dot(window, weight, preferred_element_type=F32)
    half, width = both.shape[0] // 2, both.shape[1] // 2
    rr, ri = both[:half, :width], both[:half, width:]
    ir, ii = both[half:, :width], both[half:, width:]
    if conj:
        out = [rr + ii, ir - ri]
    else:
        out = [rr - ii, ri + ir]
    return jnp.concatenate(out, 0).astype(BF16)


def kernel(
    dims,
    inv, coup, left, right, pot, pattern, fermi, eidx, own_row,
    gout, rows_out,
    ginv, gturn, xf, gf, xs, mf, mb, bb, stage, resp, sel, picked, sb, rb,
    inv_sem, fs, fr, bs, br, cs, cr, ls, ts, tr,
):
    S, Q, E, W, NB, BW, NG, GB = dims
    s = lax.axis_index("slab")
    q = lax.axis_index("orb")
    rows = xf.shape[1]
    first, last = s == 0, s == S - 1
    low, high = q == 0, q == Q - 1

    def to(src, dst, ssem, rsem, ds, dq):
        return pltpu.make_async_remote_copy(
            src_ref=src, dst_ref=dst, send_sem=ssem, recv_sem=rsem,
            device_id={"slab": s + ds, "orb": q + dq},
            device_id_type=pl.DeviceIdType.MESH,
        )

    def here(src, dst, sem):
        return pltpu.make_async_copy(src, dst, sem)

    def inv_copy(e):
        return here(inv.at[e], ginv.at[e], inv_sem.at[e])

    pieces = [(0, 0, GB)]
    for g in range(1, NG):
        pieces += [(g, g * GB, BW), (g, g * GB + BW, GB - BW)]
    NP = len(pieces)

    def main(buf, e, p):
        return buf.at[e, :, pl.ds(BW + pieces[p][1], pieces[p][2])]

    def cut(src, e, p):
        return src.at[e, :, pl.ds(pieces[p][1], pieces[p][2])]

    def halo(buf, e, side):
        return buf.at[e, :, pl.ds(0 if side == 0 else BW + W, BW)]

    def edge(src, e, side):
        return src.at[e, :, pl.ds(0 if side == 0 else W - BW, BW)]

    early = s < 2

    def coupling_copies():
        out = [(None, to(mb.at[:, 1], bb.at[:, 1], cs.at[0], cr.at[0], -1, 0))]
        n = NB - 1
        out.append((None, to(mb.at[pl.ds(1, n), 0], bb.at[pl.ds(0, n), 2], cs.at[1], cr.at[1], -1, 0)))
        out.append((None, to(mb.at[pl.ds(0, n), 2], bb.at[pl.ds(1, n), 0], cs.at[2], cr.at[2], -1, 0)))
        out.append((~low, to(mb.at[0, 0], bb.at[NB - 1, 2], cs.at[3], cr.at[3], -1, -1)))
        out.append((~high, to(mb.at[NB - 1, 2], bb.at[0, 0], cs.at[4], cr.at[4], -1, 1)))
        return out

    def wave_copies(src, dst, e, ssem, rsem, ds):
        out = [(~high, NG - 1, to(edge(src, e, 1), halo(dst, e, 0), ssem.at[e, NP + 1], rsem.at[e, NP], ds, 1))]
        for p in range(NP):
            out.append((None, pieces[p][0], to(cut(src, e, p), main(dst, e, p), ssem.at[e, p], rsem.at[e, p], ds, 0)))
        out.append((~low, 0, to(edge(src, e, 0), halo(dst, e, 1), ssem.at[e, NP], rsem.at[e, NP + 1], ds, -1)))
        return out

    def lead_copies(e):
        return [
            (~low, to(edge(left, e, 0), halo(xf, e, 1), ls.at[e, 0], fr.at[e, NP + 1], 0, -1)),
            (~high, to(edge(left, e, 1), halo(xf, e, 0), ls.at[e, 1], fr.at[e, NP], 0, 1)),
        ]

    def guarded(cond, act):
        if cond is None:
            act()
        else:
            pl.when(cond)(act)

    def await_pieces(buf, e, rsem, g):
        need = [2 * g] + ([2 * g + 1] if g + 1 < NG else [])
        for p in need:
            here(main(buf, e, p), main(buf, e, p), rsem.at[e, p]).wait()

    def await_halos(buf, e, rsem, g):
        for side, at, edge_here in ((0, 0, low), (1, NG - 1, high)):
            if g == at:
                h = halo(buf, e, side)
                pl.when(~edge_here)(lambda h=h, side=side: here(h, h, rsem.at[e, NP + side]).wait())

    def each_energy(body):
        def step(e, carry):
            body(e)
            return carry

        lax.fori_loop(0, E, step, 0)

    @each_energy
    def _(e):
        inv_copy(e).start()

    @pl.when(first)
    def _():
        @each_energy
        def _(e):
            for p in range(NP):
                here(cut(left, e, p), main(xf, e, p), fr.at[e, p]).start()
            for cond, copy in lead_copies(e):
                guarded(cond, copy.start)

    @pl.when(last)
    def _():
        @each_energy
        def _(e):
            for p in range(NP):
                here(cut(right, e, p), main(gf, e, p), br.at[e, p]).start()

    def mask_row(r, carry):
        for d in range(3):
            present = pattern[r * 3 + d].astype(F32)
            for c in range(2):
                block = (coup[c, r, d].astype(F32) * present).astype(BF16)
                mb[r, d, :, pl.ds(c * BW, BW)] = block
                mf[r, d, :, pl.ds(c * BW, BW)] = block.T
        return carry

    lax.fori_loop(0, NB, mask_row, 0)

    @pl.when(~first)
    def _():
        for cond, copy in coupling_copies():
            guarded(cond, copy.start)

    def turn_inverses(e):
        def turn(k, carry):
            gturn[e, k // NG, k % NG] = ginv[e, k // NG, k % NG].T
            return carry

        lax.fori_loop(0, 2 * NG, turn, 0)

    zero = jnp.zeros((E, rows, BW), BF16)
    zero_block = jnp.zeros((BW, 2 * BW), BF16)

    @pl.when(low)
    def _():
        xf[:, :, pl.ds(0, BW)] = zero
        gf[:, :, pl.ds(0, BW)] = zero
        bb[0, 0] = zero_block

    @pl.when(high)
    def _():
        xf[:, :, pl.ds(BW + W, BW)] = zero
        gf[:, :, pl.ds(BW + W, BW)] = zero
        bb[NB - 1, 2] = zero_block

    resp[...] = jnp.zeros(resp.shape, F32)

    atoms = own_row.shape[1]
    earlier = lax.broadcasted_iota(jnp.int32, (atoms, atoms), 0) < lax.broadcasted_iota(jnp.int32, (atoms, atoms), 1)
    eye = lax.broadcasted_iota(jnp.int32, (atoms, atoms), 0) == lax.broadcasted_iota(jnp.int32, (atoms, atoms), 1)
    own_col = jnp.sum(jnp.where(eye, own_row[...].astype(F32), 0.0), 1, keepdims=True)
    same = own_col == own_row[...].astype(F32)
    rank = jnp.sum((same & earlier).astype(F32), 0, keepdims=True)
    place = lax.broadcasted_iota(jnp.int32, (S * SCAP, atoms), 0)
    rank_i = rank.astype(jnp.int32)
    wanted = own_row[...] * SCAP + rank_i
    sel[...] = jnp.where(place == wanted, 1.0, 0.0).astype(BF16)

    def born(e, raw, g):
        held = ginv if raw else gturn
        dn = (((1,), (1 if raw else 0,)), ((), ()))

        def through(u):
            return lax.dot_general(u, held[e, 0, g], dn, preferred_element_type=F32) + lax.dot_general(
                turned(u, False), held[e, 1, g], dn, preferred_element_type=F32
            )

        u = stage[:, pl.ds(g * GB, GB)]
        gain = through(u).astype(BF16).astype(F32)
        mix = (u.astype(F32) + pot[:, pl.ds(g * GB, GB)] * gain).astype(BF16)
        return through(mix)

    def couple(buf, e, weights, g, conj):
        per = GB // BW
        for b in range(g * per, (g + 1) * per):
            window = buf[e, :, pl.ds(b * BW, 3 * BW)]
            stage[:, pl.ds(b * BW, BW)] = coupled(window, weights[b].reshape(3 * BW, 2 * BW), conj)

    def send(copies, g, cond):
        @pl.when(cond)
        def _():
            for c, after, copy in copies:
                if after == g:
                    guarded(c, copy.start)

    @pl.when(~early)
    def _():
        @each_energy
        def _(e):
            inv_copy(e).wait()
            turn_inverses(e)

    def forward(e, raw):
        if raw:
            inv_copy(e).wait()
        copies = wave_copies(xs, xf, e, fs, fr, 1)
        for g in range(NG):
            await_pieces(xf, e, fr, g)
            await_halos(xf, e, fr, g)
            couple(xf, e, mf, g, False)
            xs[e, :, pl.ds(g * GB, GB)] = born(e, raw, g).astype(BF16)
            send(copies, g, ~last)

    def backward(e):
        @pl.when(~last & (e == 0))
        def _():
            for i, region in enumerate((bb.at[:, 1], bb.at[pl.ds(0, NB - 1), 2], bb.at[pl.ds(1, NB - 1), 0])):
                here(region, region, cr.at[i]).wait()
            pl.when(~high)(lambda: here(bb.at[NB - 1, 2], bb.at[NB - 1, 2], cr.at[3]).wait())
            pl.when(~low)(lambda: here(bb.at[0, 0], bb.at[0, 0], cr.at[4]).wait())

        copies = wave_copies(gout, gf, e, bs, br, -1)
        for g in range(NG):
            cols = pl.ds(g * GB, GB)
            await_pieces(gf, e, br, g)

            @pl.when(last)
            def _():
                stage[:, cols] = gf[e, :, pl.ds(BW + g * GB, GB)]

            @pl.when(~last)
            def _():
                await_halos(gf, e, br, g)
                couple(gf, e, bb, g, True)

            gout[e, :, cols] = (xs[e, :, cols].astype(F32) + born(e, False, g)).astype(BF16)
            send(copies, g, ~first)

        weight = fermi[eidx[e]]
        for b in range(NB):
            a = gout[e, :, pl.ds(b * BW, BW)]
            gram = lax.dot_general(a, a, (((0,), (0,)), ((), ())), preferred_element_type=F32)
            resp[pl.ds(b * BW, BW), :] += weight * gram

    lag = jnp.where(last, 0, jnp.where(s == S - 2, min(LAG, E), E))

    def slot(t, carry):
        e = lax.rem(t, E)
        pl.when((t < E) & early)(lambda: forward(e, True))
        pl.when((t < E) & ~early)(lambda: forward(e, False))
        pl.when((t == E) & early)(lambda: each_energy(turn_inverses))
        pl.when((t >= lag) & (t < lag + E))(lambda: backward(lax.rem(t + 2 * E - lag, E)))
        return carry

    lax.fori_loop(0, 2 * E, slot, 0)

    for x in range(ATOM_ORB):
        part = (resp[pl.ds(x, atoms, stride=ATOM_ORB), :] * (1.0 / rows)).astype(BF16)
        picked[pl.ds(x, S * SCAP, stride=ATOM_ORB), :] = jnp.dot(sel[...], part, preferred_element_type=F32)
    sb[...] = picked[...].reshape(sb.shape).astype(BF16)

    def tail(k):
        other = lax.rem(s + k, S)
        return pltpu.make_async_remote_copy(
            src_ref=sb.at[other], dst_ref=rb.at[s], send_sem=ts.at[k], recv_sem=tr.at[k],
            device_id={"slab": other, "orb": q}, device_id_type=pl.DeviceIdType.MESH,
        )

    for k in range(1, S):
        tail(k).start()
    rb[s] = sb[s]

    @pl.when(~first)
    def _():
        for cond, copy in coupling_copies():
            guarded(cond, copy.wait_send)

        @each_energy
        def _(e):
            for cond, _, copy in wave_copies(gout, gf, e, bs, br, -1):
                guarded(cond, copy.wait_send)

    @pl.when(first)
    def _():
        @each_energy
        def _(e):
            for cond, copy in lead_copies(e):
                guarded(cond, copy.wait_send)

    @pl.when(~last)
    def _():
        @each_energy
        def _(e):
            for cond, _, copy in wave_copies(xs, xf, e, fs, fr, 1):
                guarded(cond, copy.wait_send)

    for k in range(1, S):
        tail(k).wait_send()
    for k in range(1, S):
        source = lax.rem(s + S - k, S)
        here(rb.at[source], rb.at[source], tr.at[k]).wait()
    rows_out[...] = rb[...].astype(F32)


def shards(
    inverses, coupling, pattern, left_lead, right_lead, potential, fermi_weight, energy_index, owner_map
):
    S, Q = lax.axis_size("slab"), lax.axis_size("orb")
    E, _, modes, W = left_lead.shape
    NB, BW = coupling.shape[2], coupling.shape[-1]
    NG, GB = inverses.shape[3], inverses.shape[4]
    rows = 2 * modes
    atoms = owner_map.shape[1]
    owners = owner_map.reshape(atoms)
    vm = pl.BlockSpec(memory_space=pltpu.VMEM)
    sm = pl.BlockSpec(memory_space=pltpu.SMEM)
    hbm = pl.BlockSpec(memory_space=pl.ANY)
    dma = pltpu.SemaphoreType.DMA
    green, received = pl.pallas_call(
        functools.partial(kernel, (S, Q, E, W, NB, BW, NG, GB)),
        out_shape=(
            jax.ShapeDtypeStruct((E, rows, W), BF16),
            jax.ShapeDtypeStruct((S, SCAP * ATOM_ORB, BW), F32),
        ),
        in_specs=[hbm, vm, hbm, hbm, vm, sm, sm, sm, vm],
        out_specs=(vm, vm),
        scratch_shapes=[
            pltpu.VMEM((E, 2, NG, GB, GB), BF16),
            pltpu.VMEM((E, 2, NG, GB, GB), BF16),
            pltpu.VMEM((E, rows, W + 2 * BW), BF16),
            pltpu.VMEM((E, rows, W + 2 * BW), BF16),
            pltpu.VMEM((E, rows, W), BF16),
            pltpu.VMEM((NB, 3, BW, 2 * BW), BF16),
            pltpu.VMEM((NB, 3, BW, 2 * BW), BF16),
            pltpu.VMEM((NB, 3, BW, 2 * BW), BF16),
            pltpu.VMEM((rows, W), BF16),
            pltpu.VMEM((W, BW), F32),
            pltpu.VMEM((S * SCAP, atoms), BF16),
            pltpu.VMEM((S * SCAP * ATOM_ORB, BW), F32),
            pltpu.VMEM((S, SCAP * ATOM_ORB, BW), BF16),
            pltpu.VMEM((S, SCAP * ATOM_ORB, BW), BF16),
            dma((E,)),
            dma((E, 2 * NG + 1)),
            dma((E, 2 * NG + 1)),
            dma((E, 2 * NG + 1)),
            dma((E, 2 * NG + 1)),
            dma((5,)),
            dma((5,)),
            dma((E, 2)),
            dma((S,)),
            dma((S,)),
        ],
        compiler_params=pltpu.CompilerParams(has_side_effects=True, vmem_limit_bytes=60 * 2**20),
    )(
        inverses[0],
        coupling[0],
        left_lead.reshape(E, rows, W),
        right_lead.reshape(E, rows, W),
        potential,
        pattern.reshape(NB * 3),
        fermi_weight,
        energy_index,
        owners.reshape(1, atoms),
    )
    return (
        green.reshape(1, E, 2, modes, W),
        received.reshape(1, S, SCAP, ATOM_ORB, BW),
    )


def solution(mesh):
    in_specs = (
        P("slab", None, None, "orb", None, None),
        P("slab", None, "orb", None, None, None),
        P("slab", "orb", None),
        P(None, None, None, "orb"),
        P(None, None, None, "orb"),
        P("slab", "orb"),
        P(),
        P(),
        P("slab", "orb", None),
    )
    out_specs = (P("slab", None, None, None, "orb"), P("slab", None, "orb", None, None))
    return jax.shard_map(shards, mesh=mesh, in_specs=in_specs, out_specs=out_specs, check_vma=False)
```
